512 devices in a mesh: seq: 8 (over z_hi, core), ffn: 64 (over x, z_lo, y).
Axes of the slice: x: 4, y: 4, z: 16 (z_hi: 4, z_lo: 4; z = z_hi * 4 + z_lo), core: 2. Of those that a mesh axis runs over, the one named last changes fastest.
Arguments:
- teacher_rows: bfloat16 [1024, 4096], P('ffn', 'seq'), may hold values from -6 to 6
- grad_out: bfloat16 [1024, 4096], P('ffn', 'seq'), may hold values from -0.1875 to 0.1875
- w_gate: bfloat16 [4096, 16384], P('seq', 'ffn'), may hold values from -0.125 to 0.125
- w_up: bfloat16 [4096, 16384], P('seq', 'ffn'), may hold values from -0.125 to 0.125
- w_down: bfloat16 [16384, 4096], P('ffn', 'seq'), may hold values from -0.0625 to 0.0625
- mask_gate: int32 [32, 128], P('seq', 'ffn'), may hold values from 0 to 1, as said below
- mask_up: int32 [32, 128], P('seq', 'ffn'), may hold values from 0 to 1, as said below
- mask_down: int32 [128, 32], P('ffn', 'seq'), may hold values from 0 to 1, as said below
Outputs:
- layer_out: bfloat16 [1024, 4096], P('ffn', 'seq')
- grad_gate: float32 [4096, 16384], P('seq', 'ffn')
- grad_up: float32 [4096, 16384], P('seq', 'ffn')
- grad_down: float32 [16384, 4096], P('ffn', 'seq')
The draws below stay inside these ranges and needn't reach their ends.
Inputs may be any that keep to these rules, and one draw needn't show every extreme that they name: `mask_gate`: each block is kept (1) or dropped (0); the share of kept blocks differs from one column of blocks to another. `mask_up`: each block is kept (1) or dropped (0); the share of kept blocks differs from one column of blocks to another. `mask_down`: each block is kept (1) or dropped (0); the share of kept blocks differs from one row of blocks to another.
All inputs are finite; a program needn't handle non-finite values.
Results may differ from the reference program's by a relative error of at most 0.027.
Values may be sent and summed in bfloat16 or wider, within the bound.
A program may use at most 64 MiB of HBM per device.

```python
import jax
import jax.numpy as jnp
from jax import lax

D = 4096
FF = 16384
BLK = 128
ROWS = 1024
N_SEQ = 8


def block_pattern(key, height, breadth, by_column):
    first = jax.random.fold_in(key, 11)
    second = jax.random.fold_in(key, 23)
    if by_column:
        threshold = jax.random.randint(first, (1, breadth), 30, 71)
    else:
        threshold = jax.random.randint(first, (height, 1), 30, 71)
    scores = jax.random.randint(second, (height, breadth), 0, 100)
    return (scores < threshold).astype(jnp.int32)


def draw_mask_gate(key, part):
    return block_pattern(jax.random.fold_in(key, 1), D // BLK, FF // BLK, True)


def draw_mask_up(key, part):
    return block_pattern(jax.random.fold_in(key, 2), D // BLK, FF // BLK, True)


def draw_mask_down(key, part):
    return block_pattern(jax.random.fold_in(key, 3), FF // BLK, D // BLK, False)


def block_levels(stream_key, shape, pieces, least, largest):
    level, own = 1.0, jax.random.fold_in(stream_key, 6)
    for axis_at, shards_of in pieces:
        steps = jnp.exp(jax.random.uniform(jax.random.fold_in(own, axis_at), (shards_of,), jnp.float32, least / len(pieces), largest / len(pieces)))
        level = level * jnp.repeat(steps, shape[axis_at] // shards_of).reshape([-1 if axis == axis_at else 1 for axis in range(len(shape))])
    return level


def bell_draw(key, shape, scale, most, split=(), held_as=jnp.bfloat16):
    result = jax.random.normal(key, shape, jnp.float32) * scale
    if len(split) > 0:
        result = block_levels(key, shape, split, -0.22, 0.18) * result
    return jnp.clip(result, min=-most, max=most).astype(held_as)


def setup_inputs(seed: int = 0) -> dict:
    key_of = jax.random.split(jax.random.key(seed), 9)
    return {
        "teacher_rows": bell_draw(key_of[0], (ROWS, D), 1.0, 6.0, ((0, 64), (1, 8))),
        "grad_out": bell_draw(key_of[1], (ROWS, D), (ROWS ** -0.5), 0.1875, ((0, 64), (1, 8))),
        "w_gate": bell_draw(key_of[2], (D, FF), (D // 2) ** -0.5, 0.125, ((0, 8), (1, 64))),
        "w_up": bell_draw(key_of[3], (D, FF), (D // 2) ** -0.5, 0.125, ((0, 8), (1, 64))),
        "w_down": bell_draw(key_of[4], (FF, D), (FF // 2) ** -0.5, 0.0625, ((0, 64), (1, 8))),
        "mask_gate": draw_mask_gate(jax.random.fold_in(key_of[8], 71), 0),
        "mask_up": draw_mask_up(jax.random.fold_in(key_of[8], 71), 0),
        "mask_down": draw_mask_down(jax.random.fold_in(key_of[8], 71), 0),
    }


def keep_blocks(weight, block_mask):
    height, breadth = weight.shape
    tiles = weight.reshape(height // BLK, BLK, breadth // BLK, BLK)
    kept = tiles * block_mask.astype(weight.dtype)[:, None, :, None]
    return kept.reshape(height, breadth)


def sliced_sum(left, right):
    features = left.shape[1]
    width = features // N_SEQ
    total = jnp.zeros((left.shape[0], right.shape[1]), jnp.float32)
    for index in range(N_SEQ):
        partial_value = jnp.dot(left[:, index * width:(index + 1) * width], right[index * width:(index + 1) * width, :], preferred_element_type=jnp.float32)
        rounded = lax.optimization_barrier(partial_value.astype(jnp.bfloat16))
        total = total + rounded.astype(jnp.float32)
    return total


def reference(teacher_rows, grad_out, w_gate, w_up, w_down, mask_gate, mask_up, mask_down):
    gate_kept = keep_blocks(w_gate, mask_gate)
    up_kept = keep_blocks(w_up, mask_up)
    down_kept = keep_blocks(w_down, mask_down)
    gate = sliced_sum(teacher_rows, gate_kept)
    up = sliced_sum(teacher_rows, up_kept)
    sigmoid = jax.nn.sigmoid(gate)
    active = gate * sigmoid
    hidden = (active * up).astype(jnp.bfloat16)
    layer_out = jnp.dot(hidden, down_kept, preferred_element_type=jnp.float32).astype(jnp.bfloat16)
    d_hidden = sliced_sum(grad_out, down_kept.T)
    d_gate = (d_hidden * up * sigmoid * (1.0 + gate * (1.0 - sigmoid))).astype(jnp.bfloat16)
    d_up = (d_hidden * active).astype(jnp.bfloat16)
    grad_down = keep_blocks(jnp.dot(hidden.T, grad_out, preferred_element_type=jnp.float32), mask_down)
    grad_gate = keep_blocks(jnp.dot(teacher_rows.T, d_gate, preferred_element_type=jnp.float32), mask_gate)
    grad_up = keep_blocks(jnp.dot(teacher_rows.T, d_up, preferred_element_type=jnp.float32), mask_up)
    return layer_out, grad_gate, grad_up, grad_down
```

```python
import jax
import jax.numpy as jnp
from jax import lax
from jax.experimental import pallas as pl
from jax.experimental.pallas import tpu as pltpu
from jax.sharding import PartitionSpec as P

BF = jnp.bfloat16
F32 = jnp.float32
MESH = pl.DeviceIdType.MESH
RELATIONS = (0, 1, 2, 3)


def partner(i, relation):
    if relation == 0:
        return i
    if relation == 1:
        return lax.rem(5 - i, 4)
    if relation == 2:
        return 3 - i
    return lax.rem(i + 2, 4)


def rows16(y):
    return pl.ds(pl.multiple_of(y * 16, 16), 16)


def matmul(left, right):
    return jnp.dot(left, right, preferred_element_type=F32)


def kernel(
    t_ref, g_ref, wg_ref, wu_ref, wd_ref, mg_ref, mu_ref, md_ref,
    out_ref, gg_ref, gu_ref, gd_ref,
    xf, xt, gf, wgu, wd,
    gu_send, gu_keep, gu_core, gu_zs, gu_zk, gu_r1, gu_z2, gu_r2, gu_own,
    dh_send, dh_keep, dh_core, dh_zs, dh_zk, dh_r1, dh_z2, dh_r2,
    hf, df,
    oa_own, oa_send, oa_recv, ob_own, ob_send, ob_recv,
    a2_own, a2_send, a2_recv, b2_own, b2_send, b2_recv, o3, o3_send, o3_recv,
    send_sem, recv_sem,
):
    seq = lax.axis_index("seq")
    ffn = lax.axis_index("ffn")
    zh, core = seq // 2, lax.rem(seq, 2)
    x, zl, y = ffn // 16, lax.rem(ffn // 4, 4), lax.rem(ffn, 4)
    other = 1 - core

    def ffn_peer(rx, rz, ry):
        return (seq, partner(x, rx) * 16 + partner(zl, rz) * 4 + partner(y, ry))

    def zh_peer(relation):
        return (partner(zh, relation) * 2 + core, ffn)

    core_peer = (zh * 2 + other, ffn)

    plane = [(0, rz, ry) for rz in RELATIONS for ry in RELATIONS if (rz, ry) != (0, 0)]
    peers = [ffn_peer(*r) for r in plane] + [ffn_peer(m, 0, 0) for m in (1, 2, 3)]
    peers += [core_peer, zh_peer(1), zh_peer(2)]
    barrier = pltpu.get_barrier_semaphore()
    for peer in peers:
        pl.semaphore_signal(barrier, inc=1, device_id=peer, device_id_type=MESH)

    started = []

    def send(src, dst, peer):
        index = len(started)
        copy = pltpu.make_async_remote_copy(
            src_ref=src, dst_ref=dst, send_sem=send_sem.at[index], recv_sem=recv_sem.at[index],
            device_id=peer, device_id_type=MESH,
        )
        copy.start()
        started.append(copy)
        return copy

    for a in range(4):
        for b in range(2):
            r, c = pl.ds(a * 128, 128), pl.ds(b * 128, 128)
            wgu[r, c] = (wg_ref[r, c].astype(F32) * mg_ref[a, b].astype(F32)).astype(BF)
            wgu[r, pl.ds(256 + b * 128, 128)] = (
                wu_ref[r, c].astype(F32) * mu_ref[a, b].astype(F32)
            ).astype(BF)
            wd[c, r] = (wd_ref[c, r].astype(F32) * md_ref[b, a].astype(F32)).astype(BF)
    xf[x, zl, rows16(y), :] = t_ref[...]
    gf[x, zl, rows16(y), :] = g_ref[...]

    pl.semaphore_wait(barrier, len(peers))

    x_plane = [send(t_ref, xf.at[x, zl, rows16(y)], ffn_peer(*r)) for r in plane]
    g_z = [send(g_ref, gf.at[x, zl, rows16(y)], ffn_peer(0, r, 0)) for r in (1, 2, 3)]

    for copy in g_z:
        copy.wait_recv()
    g_block = gf.at[x, :, rows16(y)]
    g_x = [send(g_block, g_block, ffn_peer(r, 0, 0)) for r in (1, 2, 3)]
    for copy in x_plane:
        copy.wait_recv()
    x_copies = [None] + [send(xf.at[x], xf.at[x], ffn_peer(r, 0, 0)) for r in (1, 2, 3)]

    gu = dict(send=gu_send, keep=gu_keep, core=gu_core, zs=gu_zs, zk=gu_zk, r1=gu_r1, z2=gu_z2,
              r2=gu_r2, n=2, c1={}, c2={}, c3={})
    dh = dict(send=dh_send, keep=dh_keep, core=dh_core, zs=dh_zs, zk=dh_zk, r1=dh_r1, z2=dh_z2,
              r2=dh_r2, n=1, c1={}, c2={}, c3={})

    def to_core(k, j, parts):
        for t, part in enumerate(parts):
            low, high = part[:, :128], part[:, 128:]
            mine = jnp.where(core == 0, low, high).reshape(4, 64, 128)
            theirs = jnp.where(core == 0, high, low).reshape(4, 64, 128)
            k["send"][j, t] = theirs.astype(BF)
            k["keep"][j, t] = mine
        k["c1"][j] = send(k["send"].at[j], k["core"].at[j], core_peer)

    def to_z1(k, j):
        k["c1"][j].wait_recv()
        k["c2"][j] = []
        for h in (0, 1):
            r = pl.ds(32 * h, 32)
            first, second = (1, 2) if h == 0 else (2, 1)
            for t in range(k["n"]):
                for slot, (keep, relation) in enumerate(
                    ((False, first), (False, 3), (True, 0), (True, second))
                ):
                    b = partner(zh, relation)
                    value = k["keep"][j, t, b, r, :] + k["core"][j, t, b, r, :].astype(F32)
                    if keep:
                        k["zk"][j, h, t, slot - 2] = value
                    else:
                        k["zs"][j, h, t, slot] = value.astype(BF)
            k["c2"][j].append(send(k["zs"].at[j, h], k["r1"].at[j, h], zh_peer(first)))

    def to_z2(k, j):
        k["c3"][j] = []
        for h in (0, 1):
            k["c2"][j][h].wait_recv()
            for t in range(k["n"]):
                k["z2"][j, h, t] = (k["zk"][j, h, t, 1] + k["r1"][j, h, t, 1].astype(F32)).astype(BF)
            k["c3"][j].append(send(k["z2"].at[j, h], k["r2"].at[j, h], zh_peer(2 if h == 0 else 1)))

    def owned(k, j, h, t):
        return (
            k["zk"][j, h, t, 0] + k["r1"][j, h, t, 0].astype(F32) + k["r2"][j, h, t].astype(F32)
        )

    def gather1(full, j):
        mine = full.at[j, core, :, zh]
        return [send(mine, mine, zh_peer(r)) for r in (1, 2)]

    def gather2(full, j, copies):
        result = []
        for h, (relation, onward) in enumerate(((1, 2), (2, 1))):
            copies[h].wait_recv()
            block = full.at[j, core, :, partner(zh, relation), pl.ds(32 * h, 32)]
            result.append(send(block, block, zh_peer(onward)))
        return result

    def gather3(full, j, copies):
        for copy in copies:
            copy.wait_recv()
        return send(full.at[j, core], full.at[j, core], core_peer)

    def gu_compute(j):
        if j:
            x_copies[j].wait_recv()
        chunk = xf[partner(x, j)].reshape(256, 512)
        both = matmul(chunk, wgu[...])
        to_core(gu, j, [both[:, :256], both[:, 256:]])

    def transpose_x(j):
        xt[j] = xf[partner(x, j)].reshape(256, 512).T

    h1, h2, h3, d1, d2, d3 = ({} for _ in range(6))

    def gu_final(j):
        for h in (0, 1):
            gu["c3"][j][h].wait_recv()
            gate, up = owned(gu, j, h, 0), owned(gu, j, h, 1)
            sig = 1.0 / (1.0 + jnp.exp(-gate))
            hf[j, core, 0, zh, pl.ds(32 * h, 32), :] = (gate * sig * up).astype(BF)
            gu_own[j, h, 0] = gate
            gu_own[j, h, 1] = up
        h1[j] = gather1(hf, j)

    def dh_compute(j):
        chunk = gf[partner(x, j)].reshape(256, 512)
        to_core(dh, j, [lax.dot_general(chunk, wd[...], (((1,), (1,)), ((), ())), preferred_element_type=F32)])

    def dh_final(j):
        for h in (0, 1):
            dh["c3"][j][h].wait_recv()
            d_hidden, gate, up = owned(dh, j, h, 0), gu_own[j, h, 0], gu_own[j, h, 1]
            sig = 1.0 / (1.0 + jnp.exp(-gate))
            d_gate = d_hidden * up * sig * (1.0 + gate * (1.0 - sig))
            d_up = d_hidden * (gate * sig)
            df[j, core, 0, zh, pl.ds(32 * h, 32), :] = d_gate.astype(BF)
            df[j, core, 1, zh, pl.ds(32 * h, 32), :] = d_up.astype(BF)
        d1[j] = gather1(df, j)

    def h_go2(j):
        h2[j] = gather2(hf, j, h1[j])

    def h_go3(j):
        h3[j] = gather3(hf, j, h2[j])

    def d_go2(j):
        d2[j] = gather2(df, j, d1[j])

    def d_go3(j):
        d3[j] = gather3(df, j, d2[j])

    oa, ob = {}, {}

    def h_final(j):
        h3[j].wait_recv()
        hidden = jnp.concatenate(
            [hf[j, 0, 0].reshape(256, 128), hf[j, 1, 0].reshape(256, 128)], axis=1
        )
        part = matmul(hidden, wd[...])
        a, b = part[:, :256].reshape(4, 64, 256), part[:, 256:].reshape(4, 64, 256)
        if j == 0:
            oa_own[...] = a
        else:
            oa_send[j - 1] = a.astype(BF)
            oa[j] = send(oa_send.at[j - 1], oa_recv.at[j - 1], ffn_peer(j, 0, 0))
        ob_send[j] = b.astype(BF)
        ob[j] = [
            send(ob_send.at[j, :, rows16(partner(y, r))], ob_recv.at[j, r - 1], ffn_peer(0, 0, r))
            for r in (1, 2, 3)
        ]
        chunk = gf[partner(x, j)].reshape(256, 512)
        term = lax.dot_general(hidden, chunk, (((0,), (0,)), ((), ())), preferred_element_type=F32)
        if j == 0:
            gd_ref[...] = term
        else:
            gd_ref[...] += term

    a2, b2, z3 = {}, {}, {}

    def out_second():
        for j in (1, 2, 3):
            oa[j].wait_recv()
        total = oa_own[...]
        for j in range(3):
            total += oa_recv[j].astype(F32)
        oa_own[...] = total
        a2_send[...] = total.astype(BF)
        for r in (1, 2, 3):
            a2[r] = send(a2_send.at[:, rows16(partner(y, r))], a2_recv.at[r - 1], ffn_peer(0, 0, r))
        for j in range(4):
            for copy in ob[j]:
                copy.wait_recv()
            total = ob_send[j, :, rows16(y), :].astype(F32)
            for r in range(3):
                total += ob_recv[j, r].astype(F32)
            if j == 0:
                b2_own[...] = total
            else:
                b2_send[j - 1] = total.astype(BF)
                b2[j] = send(b2_send.at[j - 1], b2_recv.at[j - 1], ffn_peer(j, 0, 0))

    def out_third():
        for r in (1, 2, 3):
            a2[r].wait_recv()
            b2[r].wait_recv()
        left, right = oa_own[:, rows16(y), :], b2_own[...]
        for r in range(3):
            left += a2_recv[r].astype(F32)
            right += b2_recv[r].astype(F32)
        o3[:, :, :256] = left
        o3[:, :, 256:] = right
        o3_send[...] = o3[...].astype(BF)
        for r in (1, 2, 3):
            z3[r] = send(o3_send.at[partner(zl, r)], o3_recv.at[r - 1], ffn_peer(0, r, 0))

    def out_final():
        total = o3[zl]
        for r in (1, 2, 3):
            z3[r].wait_recv()
            total += o3_recv[r - 1].astype(F32)
        out_ref[...] = total.astype(BF)

    def d_final(j):
        d3[j].wait_recv()
        for t, ref in enumerate((gg_ref, gu_ref)):
            grad = jnp.concatenate(
                [df[j, 0, t].reshape(256, 128), df[j, 1, t].reshape(256, 128)], axis=1
            )
            term = matmul(xt[j], grad)
            if j == 0:
                ref[...] = term
            else:
                ref[...] += term

    def g_to_y():
        for copy in g_x:
            copy.wait_recv()
        column = gf.at[:, :, rows16(y)]
        return [send(column, column, ffn_peer(0, 0, r)) for r in (1, 2, 3)]

    gu_compute(0)
    g_y = g_to_y()
    to_z1(gu, 0)
    transpose_x(0)
    gu_compute(1)
    to_z1(gu, 1)
    to_z2(gu, 0)
    transpose_x(1)
    gu_compute(2)
    to_z1(gu, 2)
    to_z2(gu, 1)
    gu_final(0)
    transpose_x(2)
    gu_compute(3)
    to_z1(gu, 3)
    to_z2(gu, 2)
    gu_final(1)
    transpose_x(3)
    for copy in g_y:
        copy.wait_recv()
    dh_compute(0)
    dh_compute(1)
    to_z2(gu, 3)
    to_z1(dh, 0)
    dh_compute(2)
    dh_compute(3)
    h_go2(0)
    gu_final(2)
    to_z1(dh, 1)
    h_go2(1)
    gu_final(3)
    to_z1(dh, 2)
    to_z1(dh, 3)
    to_z2(dh, 0)
    h_go3(0)
    h_go2(2)
    to_z2(dh, 1)
    h_go3(1)
    h_go2(3)
    to_z2(dh, 2)
    to_z2(dh, 3)
    dh_final(0)
    h_final(0)
    dh_final(1)
    h_final(1)
    h_go3(2)
    h_go3(3)
    dh_final(2)
    d_go2(0)
    dh_final(3)
    d_go2(1)
    h_final(2)
    h_final(3)
    d_go3(0)
    d_go2(2)
    d_go3(1)
    d_go2(3)
    for a in range(2):
        for b in range(4):
            r, c = pl.ds(a * 128, 128), pl.ds(b * 128, 128)
            gd_ref[r, c] = gd_ref[r, c] * md_ref[a, b].astype(F32)
    out_second()
    d_final(0)
    d_go3(2)
    d_final(1)
    d_go3(3)
    out_third()
    d_final(2)
    d_final(3)
    for a in range(4):
        for b in range(2):
            r, c = pl.ds(a * 128, 128), pl.ds(b * 128, 128)
            gg_ref[r, c] = gg_ref[r, c] * mg_ref[a, b].astype(F32)
            gu_ref[r, c] = gu_ref[r, c] * mu_ref[a, b].astype(F32)
    out_final()
    for copy in started:
        copy.wait_send()


def reduce_scratch(n):
    return [
        pltpu.VMEM((4, n, 4, 64, 128), BF),
        pltpu.VMEM((4, n, 4, 64, 128), F32),
        pltpu.VMEM((4, n, 4, 64, 128), BF),
        pltpu.VMEM((4, 2, n, 2, 32, 128), BF),
        pltpu.VMEM((4, 2, n, 2, 32, 128), F32),
        pltpu.VMEM((4, 2, n, 2, 32, 128), BF),
        pltpu.VMEM((4, 2, n, 32, 128), BF),
        pltpu.VMEM((4, 2, n, 32, 128), BF),
    ]


COPIES = 160


def on_device(*args):
    vmem = pl.BlockSpec(memory_space=pltpu.VMEM)
    smem = pl.BlockSpec(memory_space=pltpu.SMEM)
    return pl.pallas_call(
        kernel,
        out_shape=(
            jax.ShapeDtypeStruct((16, 512), BF),
            jax.ShapeDtypeStruct((512, 256), F32),
            jax.ShapeDtypeStruct((512, 256), F32),
            jax.ShapeDtypeStruct((256, 512), F32),
        ),
        in_specs=[vmem] * 5 + [smem] * 3,
        out_specs=(vmem,) * 4,
        scratch_shapes=[
            pltpu.VMEM((4, 4, 64, 512), BF),
            pltpu.VMEM((4, 512, 256), BF),
            pltpu.VMEM((4, 4, 64, 512), BF),
            pltpu.VMEM((512, 512), BF),
            pltpu.VMEM((256, 512), BF),
            *reduce_scratch(2),
            pltpu.VMEM((4, 2, 2, 32, 128), F32),
            *reduce_scratch(1),
            pltpu.VMEM((4, 2, 1, 4, 64, 128), BF),
            pltpu.VMEM((4, 2, 2, 4, 64, 128), BF),
            pltpu.VMEM((4, 64, 256), F32),
            pltpu.VMEM((3, 4, 64, 256), BF),
            pltpu.VMEM((3, 4, 64, 256), BF),
            pltpu.VMEM((4, 16, 256), F32),
            pltpu.VMEM((4, 4, 64, 256), BF),
            pltpu.VMEM((4, 3, 4, 16, 256), BF),
            pltpu.VMEM((4, 16, 256), F32),
            pltpu.VMEM((4, 64, 256), BF),
            pltpu.VMEM((3, 4, 16, 256), BF),
            pltpu.VMEM((4, 16, 256), F32),
            pltpu.VMEM((3, 4, 16, 256), BF),
            pltpu.VMEM((3, 4, 16, 256), BF),
            pltpu.VMEM((4, 16, 512), F32),
            pltpu.VMEM((4, 16, 512), BF),
            pltpu.VMEM((3, 16, 512), BF),
            pltpu.SemaphoreType.DMA((COPIES,)),
            pltpu.SemaphoreType.DMA((COPIES,)),
        ],
        compiler_params=pltpu.CompilerParams(
            collective_id=0, has_side_effects=True, vmem_limit_bytes=48 * 2**20
        ),
        cost_estimate=pl.CostEstimate(flops=1_700_000_000, bytes_accessed=2_500_000, transcendentals=100_000),
    )(*args)


def solution(mesh):
    return jax.shard_map(
        on_device,
        mesh=mesh,
        in_specs=(
            P("ffn", "seq"),
            P("ffn", "seq"),
            P("seq", "ffn"),
            P("seq", "ffn"),
            P("ffn", "seq"),
            P("seq", "ffn"),
            P("seq", "ffn"),
            P("ffn", "seq"),
        ),
        out_specs=(P("ffn", "seq"), P("seq", "ffn"), P("seq", "ffn"), P("ffn", "seq")),
        check_vma=False,
    )
```

```python
import jax
import jax.numpy as jnp
from jax import lax
from jax.experimental import pallas as pl
from jax.experimental.pallas import tpu as pltpu
from jax.sharding import PartitionSpec as P

BF = jnp.bfloat16
F32 = jnp.float32
MESH = pl.DeviceIdType.MESH
RELATIONS = (0, 1, 2, 3)


def partner(i, relation):
    if relation == 0:
        return i
    if relation == 1:
        return lax.rem(5 - i, 4)
    if relation == 2:
        return 3 - i
    return lax.rem(i + 2, 4)


def rows16(y):
    return pl.ds(pl.multiple_of(y * 16, 16), 16)


def matmul(left, right):
    return jnp.dot(left, right, preferred_element_type=F32)


def kernel(
    t_ref, g_ref, wg_ref, wu_ref, wd_ref, mgt_ref, mut_ref, mdt_ref,
    out_ref, gg_ref, gu_ref, gd_ref,
    wg_raw, wu_raw, wd_raw, mg, mu, md, xf, xt, gf, wgu, wd, wdp,
    gu_send, gu_keep, gu_core, gu_zs, gu_zk, gu_r1, gu_z2, gu_r2, gu_own,
    dh_send, dh_keep, dh_core, dh_zs, dh_zk, dh_r1, dh_z2, dh_r2,
    hf, df,
    oa_own, oa_send, oa_recv, ob_own, ob_send, ob_recv,
    a2_own, a2_send, a2_recv, b2_own, b2_send, b2_recv, o3, o3_send, o3_recv,
    send_sem, recv_sem, load_sem,
):
    seq = lax.axis_index("seq")
    ffn = lax.axis_index("ffn")
    zh, core = seq // 2, lax.rem(seq, 2)
    x, zl, y = ffn // 16, lax.rem(ffn // 4, 4), lax.rem(ffn, 4)
    other = 1 - core

    def ffn_peer(rx, rz, ry):
        return (seq, partner(x, rx) * 16 + partner(zl, rz) * 4 + partner(y, ry))

    def zh_peer(relation):
        return (partner(zh, relation) * 2 + core, ffn)

    core_peer = (zh * 2 + other, ffn)

    peers = [ffn_peer(*r) for m in (1, 2, 3) for r in ((m, 0, 0), (0, m, 0), (0, 0, m))]
    peers += [core_peer, zh_peer(1), zh_peer(2)]
    barrier = pltpu.get_barrier_semaphore()
    for peer in peers:
        pl.semaphore_signal(barrier, inc=1, device_id=peer, device_id_type=MESH)

    started = []

    def send(src, dst, peer):
        index = len(started)
        copy = pltpu.make_async_remote_copy(
            src_ref=src, dst_ref=dst, send_sem=send_sem.at[index], recv_sem=recv_sem.at[index],
            device_id=peer, device_id_type=MESH,
        )
        copy.start()
        started.append(copy)
        return copy

    x_own, g_own = xf.at[x, zl, rows16(y)], gf.at[x, zl, rows16(y)]
    loads = [
        pltpu.make_async_copy(src, dst, load_sem.at[i])
        for i, (src, dst) in enumerate((
            (t_ref, x_own), (g_ref, g_own), (mgt_ref, mg), (mut_ref, mu), (mdt_ref, md),
            (wg_ref, wg_raw), (wu_ref, wu_raw), (wd_ref, wd_raw),
        ))
    ]
    for load in loads:
        load.start()
    for load in loads:
        load.wait()

    for b in range(2):
        place = lax.rem(b + core, 2)
        for a in range(4):
            r, c = pl.ds(a * 128, 128), pl.ds(b * 128, 128)
            for t, (raw, mask) in enumerate(((wg_raw, mg), (wu_raw, mu))):
                kept = (raw[r, c].astype(F32) * mask[b, a].astype(F32)).astype(BF)
                wgu[r, pl.ds(pl.multiple_of(place * 256 + t * 128, 128), 128)] = kept
            kept = (wd_raw[c, r].astype(F32) * md[b, a].astype(F32)).astype(BF)
            wd[c, r] = kept
            wdp[pl.ds(pl.multiple_of(place * 128, 128), 128), r] = kept

    pl.semaphore_wait(barrier, len(peers))

    def landed(*copies):
        for copy in copies:
            if not any(copy is old for old in arrived):
                arrived.append(copy)
                copy.wait_recv()

    arrived = []
    x_z = [send(x_own, x_own, ffn_peer(0, r, 0)) for r in (1, 2, 3)]
    g_z = [send(g_own, g_own, ffn_peer(0, r, 0)) for r in (1, 2, 3)]
    x_flow, g_flow = {}, {}
    left, right = pl.ds(0, 256), pl.ds(256, 256)

    def spread(column, rows, flow):
        landed(*column)
        a, b = rows.at[x, :, rows16(y), left], rows.at[x, :, rows16(y), right]
        flow["a"] = [send(a, a, ffn_peer(0, 0, r)) for r in (1, 2, 3)]
        flow["b"] = [send(b, b, ffn_peer(r, 0, 0)) for r in (1, 2, 3)]

    def complete(rows, flow):
        landed(*flow["a"])
        a, b = rows.at[x, :, :, left], rows.at[:, :, rows16(y), right]
        flow["all"] = [send(a, a, ffn_peer(r, 0, 0)) for r in (1, 2, 3)]
        landed(*flow["b"])
        flow["all"] += [send(b, b, ffn_peer(0, 0, r)) for r in (1, 2, 3)]

    gu = dict(send=gu_send, keep=gu_keep, core=gu_core, zs=gu_zs, zk=gu_zk, r1=gu_r1, z2=gu_z2,
              r2=gu_r2, n=2, c1={}, c2={}, c3={})
    dh = dict(send=dh_send, keep=dh_keep, core=dh_core, zs=dh_zs, zk=dh_zk, r1=dh_r1, z2=dh_z2,
              r2=dh_r2, n=1, c1={}, c2={}, c3={})

    def to_core(k, j, both):
        n = k["n"]
        for t in range(n):
            k["send"][j, t] = both[:, 128 * (n + t):128 * (n + t + 1)].reshape(4, 64, 128).astype(BF)
            k["keep"][j, t] = both[:, 128 * t:128 * (t + 1)].reshape(4, 64, 128)
        k["c1"][j] = send(k["send"].at[j], k["core"].at[j], core_peer)

    def to_z1(k, j):
        k["c1"][j].wait_recv()
        k["c2"][j] = []
        for h in (0, 1):
            r = pl.ds(32 * h, 32)
            first, second = (1, 2) if h == 0 else (2, 1)
            for t in range(k["n"]):
                for slot, (keep, relation) in enumerate(
                    ((False, first), (False, 3), (True, 0), (True, second))
                ):
                    b = partner(zh, relation)
                    value = k["keep"][j, t, b, r, :] + k["core"][j, t, b, r, :].astype(F32)
                    if keep:
                        k["zk"][j, h, t, slot - 2] = value
                    else:
                        k["zs"][j, h, t, slot] = value.astype(BF)
            k["c2"][j].append(send(k["zs"].at[j, h], k["r1"].at[j, h], zh_peer(first)))

    def to_z2(k, j):
        k["c3"][j] = []
        for h in (0, 1):
            k["c2"][j][h].wait_recv()
            for t in range(k["n"]):
                k["z2"][j, h, t] = (k["zk"][j, h, t, 1] + k["r1"][j, h, t, 1].astype(F32)).astype(BF)
            k["c3"][j].append(send(k["z2"].at[j, h], k["r2"].at[j, h], zh_peer(2 if h == 0 else 1)))

    def owned(k, j, h, t):
        return (
            k["zk"][j, h, t, 0] + k["r1"][j, h, t, 0].astype(F32) + k["r2"][j, h, t].astype(F32)
        )

    def gather1(full, j):
        mine = full.at[j, core, :, zh]
        return [send(mine, mine, zh_peer(r)) for r in (1, 2)]

    def gather2(full, j, copies):
        result = []
        for h, (relation, onward) in enumerate(((1, 2), (2, 1))):
            copies[h].wait_recv()
            block = full.at[j, core, :, partner(zh, relation), pl.ds(32 * h, 32)]
            result.append(send(block, block, zh_peer(onward)))
        return result

    def gather3(full, j, copies):
        for copy in copies:
            copy.wait_recv()
        return send(full.at[j, core], full.at[j, core], core_peer)

    def gu_compute(j):
        landed(*x_flow["all"])
        to_core(gu, j, matmul(xf[partner(x, j)].reshape(256, 512), wgu[...]))

    def transpose_x(j):
        xt[j] = xf[partner(x, j)].reshape(256, 512).T

    h1, h2, h3, d1, d2, d3 = ({} for _ in range(6))

    def gu_final(j):
        for h in (0, 1):
            gu["c3"][j][h].wait_recv()
            gate, up = owned(gu, j, h, 0), owned(gu, j, h, 1)
            sig = 1.0 / (1.0 + jnp.exp(-gate))
            hf[j, core, 0, zh, pl.ds(32 * h, 32), :] = (gate * sig * up).astype(BF)
            gu_own[j, h, 0] = gate
            gu_own[j, h, 1] = up
        h1[j] = gather1(hf, j)

    def dh_compute(j):
        landed(*g_flow["all"])
        chunk = gf[partner(x, j)].reshape(256, 512)
        to_core(dh, j, lax.dot_general(
            chunk, wdp[...], (((1,), (1,)), ((), ())), preferred_element_type=F32
        ))

    def dh_final(j):
        for h in (0, 1):
            dh["c3"][j][h].wait_recv()
            d_hidden, gate, up = owned(dh, j, h, 0), gu_own[j, h, 0], gu_own[j, h, 1]
            sig = 1.0 / (1.0 + jnp.exp(-gate))
            d_gate = d_hidden * up * sig * (1.0 + gate * (1.0 - sig))
            d_up = d_hidden * (gate * sig)
            df[j, core, 0, zh, pl.ds(32 * h, 32), :] = d_gate.astype(BF)
            df[j, core, 1, zh, pl.ds(32 * h, 32), :] = d_up.astype(BF)
        d1[j] = gather1(df, j)

    def h_go2(j):
        h2[j] = gather2(hf, j, h1[j])

    def h_go3(j):
        h3[j] = gather3(hf, j, h2[j])

    def d_go2(j):
        d2[j] = gather2(df, j, d1[j])

    def d_go3(j):
        d3[j] = gather3(df, j, d2[j])

    oa, ob = {}, {}
    h_done, d_done = [], []
    h_done, d_done = [], []

    def h_final(j):
        h3[j].wait_recv()
        hidden = jnp.concatenate(
            [hf[j, 0, 0].reshape(256, 128), hf[j, 1, 0].reshape(256, 128)], axis=1
        )
        part = matmul(hidden, wd[...])
        a, b = part[:, :256].reshape(4, 64, 256), part[:, 256:].reshape(4, 64, 256)
        if j == 0:
            oa_own[...] = a
        else:
            oa_send[j - 1] = a.astype(BF)
            oa[j] = send(oa_send.at[j - 1], oa_recv.at[j - 1], ffn_peer(j, 0, 0))
        ob_send[j] = b.astype(BF)
        ob[j] = [
            send(ob_send.at[j, :, rows16(partner(y, r))], ob_recv.at[j, r - 1], ffn_peer(0, 0, r))
            for r in (1, 2, 3)
        ]
        chunk = gf[partner(x, j)].reshape(256, 512)
        term = lax.dot_general(hidden, chunk, (((0,), (0,)), ((), ())), preferred_element_type=F32)
        if h_done:
            term += gd_ref[...]
        h_done.append(j)
        if len(h_done) < 4:
            gd_ref[...] = term
            return
        for a in range(2):
            for b in range(4):
                r, c = slice(a * 128, a * 128 + 128), slice(b * 128, b * 128 + 128)
                gd_ref[r, c] = term[r, c] * md[a, b].astype(F32)

    a2, b2, z3 = {}, {}, {}

    def out_second():
        for j in (1, 2, 3):
            oa[j].wait_recv()
        total = oa_own[...]
        for j in range(3):
            total += oa_recv[j].astype(F32)
        oa_own[...] = total
        a2_send[...] = total.astype(BF)
        for r in (1, 2, 3):
            a2[r] = send(a2_send.at[:, rows16(partner(y, r))], a2_recv.at[r - 1], ffn_peer(0, 0, r))
        for j in range(4):
            for copy in ob[j]:
                copy.wait_recv()
            total = ob_send[j, :, rows16(y), :].astype(F32)
            for r in range(3):
                total += ob_recv[j, r].astype(F32)
            if j == 0:
                b2_own[...] = total
            else:
                b2_send[j - 1] = total.astype(BF)
                b2[j] = send(b2_send.at[j - 1], b2_recv.at[j - 1], ffn_peer(j, 0, 0))

    def out_third():
        for r in (1, 2, 3):
            a2[r].wait_recv()
            b2[r].wait_recv()
        left, right = oa_own[:, rows16(y), :], b2_own[...]
        for r in range(3):
            left += a2_recv[r].astype(F32)
            right += b2_recv[r].astype(F32)
        o3[:, :, :256] = left
        o3[:, :, 256:] = right
        o3_send[...] = o3[...].astype(BF)
        for r in (1, 2, 3):
            z3[r] = send(o3_send.at[partner(zl, r)], o3_recv.at[r - 1], ffn_peer(0, r, 0))

    def out_final():
        total = o3[zl]
        for r in (1, 2, 3):
            z3[r].wait_recv()
            total += o3_recv[r - 1].astype(F32)
        out_ref[...] = total.astype(BF)

    def d_final(j):
        d3[j].wait_recv()
        for t, (ref, mask) in enumerate(((gg_ref, mg), (gu_ref, mu))):
            grad = jnp.concatenate(
                [df[j, 0, t].reshape(256, 128), df[j, 1, t].reshape(256, 128)], axis=1
            )
            term = matmul(xt[j], grad)
            if d_done:
                term += ref[...]
            if len(d_done) < 3:
                ref[...] = term
                continue
            for a in range(4):
                for b in range(2):
                    r, c = slice(a * 128, a * 128 + 128), slice(b * 128, b * 128 + 128)
                    ref[r, c] = term[r, c] * mask[b, a].astype(F32)
        d_done.append(j)
        d_done.append(j)

    spread(x_z, xf, x_flow)
    complete(xf, x_flow)
    gu_compute(0)
    gu_compute(1)
    gu_compute(2)
    gu_compute(3)
    spread(g_z, gf, g_flow)
    to_z1(gu, 0)
    to_z1(gu, 1)
    to_z1(gu, 2)
    to_z1(gu, 3)
    complete(gf, g_flow)
    transpose_x(0)
    transpose_x(1)
    transpose_x(2)
    transpose_x(3)
    to_z2(gu, 0)
    to_z2(gu, 1)
    to_z2(gu, 2)
    to_z2(gu, 3)
    dh_compute(0)
    dh_compute(1)
    dh_compute(2)
    dh_compute(3)
    gu_final(0)
    gu_final(1)
    to_z1(dh, 0)
    to_z1(dh, 1)
    gu_final(2)
    to_z1(dh, 2)
    gu_final(3)
    to_z1(dh, 3)
    h_go2(0)
    h_go2(1)
    h_go2(2)
    h_go2(3)
    to_z2(dh, 0)
    h_go3(0)
    to_z2(dh, 1)
    h_go3(1)
    to_z2(dh, 2)
    to_z2(dh, 3)
    h_final(0)
    h_final(1)
    h_go3(2)
    h_go3(3)
    h_final(2)
    h_final(3)
    dh_final(0)
    dh_final(1)
    dh_final(2)
    dh_final(3)
    out_second()
    d_go2(0)
    d_go2(1)
    d_go2(2)
    d_go2(3)
    out_third()
    d_go3(0)
    d_go3(1)
    d_final(0)
    d_go3(2)
    d_final(1)
    d_go3(3)
    out_final()
    d_final(2)
    d_final(3)
    for copy in started:
        copy.wait_send()


def hand_over(*refs):
    source, result, held, sem = refs[:4], refs[4:8], refs[8:12], refs[12]
    loads = [pltpu.make_async_copy(source[i], held[i], sem.at[0, i]) for i in range(4)]
    stores = [pltpu.make_async_copy(held[i], result[i], sem.at[1, i]) for i in range(4)]
    for load in loads:
        load.start()
    for load, store in zip(loads, stores):
        load.wait()
        store.start()
    for store in stores:
        store.wait()


def reduce_scratch(n):
    return [
        pltpu.VMEM((4, n, 4, 64, 128), BF),
        pltpu.VMEM((4, n, 4, 64, 128), F32),
        pltpu.VMEM((4, n, 4, 64, 128), BF),
        pltpu.VMEM((4, 2, n, 2, 32, 128), BF),
        pltpu.VMEM((4, 2, n, 2, 32, 128), F32),
        pltpu.VMEM((4, 2, n, 2, 32, 128), BF),
        pltpu.VMEM((4, 2, n, 32, 128), BF),
        pltpu.VMEM((4, 2, n, 32, 128), BF),
    ]


COPIES = 160


def on_device(teacher_rows, grad_out, w_gate, w_up, w_down, mask_gate, mask_up, mask_down):
    args = (teacher_rows, grad_out, w_gate, w_up, w_down, mask_gate.T, mask_up.T, mask_down)
    vmem = pl.BlockSpec(memory_space=pltpu.VMEM)
    hbm = pl.BlockSpec(memory_space=pltpu.HBM)
    results = pl.pallas_call(
        kernel,
        out_shape=(
            jax.ShapeDtypeStruct((16, 512), BF),
            jax.ShapeDtypeStruct((512, 256), F32),
            jax.ShapeDtypeStruct((512, 256), F32),
            jax.ShapeDtypeStruct((256, 512), F32),
        ),
        in_specs=[hbm] * 8,
        out_specs=(vmem,) * 4,
        scratch_shapes=[
            pltpu.VMEM((512, 256), BF),
            pltpu.VMEM((512, 256), BF),
            pltpu.VMEM((256, 512), BF),
            *[pltpu.SMEM((2, 4), jnp.int32)] * 3,
            pltpu.VMEM((4, 4, 64, 512), BF),
            pltpu.VMEM((4, 512, 256), BF),
            pltpu.VMEM((4, 4, 64, 512), BF),
            pltpu.VMEM((512, 512), BF),
            pltpu.VMEM((256, 512), BF),
            pltpu.VMEM((256, 512), BF),
            *reduce_scratch(2),
            pltpu.VMEM((4, 2, 2, 32, 128), F32),
            *reduce_scratch(1),
            pltpu.VMEM((4, 2, 1, 4, 64, 128), BF),
            pltpu.VMEM((4, 2, 2, 4, 64, 128), BF),
            pltpu.VMEM((4, 64, 256), F32),
            pltpu.VMEM((3, 4, 64, 256), BF),
            pltpu.VMEM((3, 4, 64, 256), BF),
            pltpu.VMEM((4, 16, 256), F32),
            pltpu.VMEM((4, 4, 64, 256), BF),
            pltpu.VMEM((4, 3, 4, 16, 256), BF),
            pltpu.VMEM((4, 16, 256), F32),
            pltpu.VMEM((4, 64, 256), BF),
            pltpu.VMEM((3, 4, 16, 256), BF),
            pltpu.VMEM((4, 16, 256), F32),
            pltpu.VMEM((3, 4, 16, 256), BF),
            pltpu.VMEM((3, 4, 16, 256), BF),
            pltpu.VMEM((4, 16, 512), F32),
            pltpu.VMEM((4, 16, 512), BF),
            pltpu.VMEM((3, 16, 512), BF),
            pltpu.SemaphoreType.DMA((COPIES,)),
            pltpu.SemaphoreType.DMA((COPIES,)),
            pltpu.SemaphoreType.DMA((8,)),
        ],
        compiler_params=pltpu.CompilerParams(
            collective_id=0, has_side_effects=True, vmem_limit_bytes=62 * 2**20
        ),
        cost_estimate=pl.CostEstimate(flops=1_700_000_000, bytes_accessed=2_500_000, transcendentals=100_000),
    )(*args)
    return pl.pallas_call(
        hand_over,
        out_shape=tuple(jax.ShapeDtypeStruct(r.shape, r.dtype) for r in results),
        in_specs=[hbm] * 4,
        out_specs=(hbm,) * 4,
        scratch_shapes=[*[pltpu.VMEM(r.shape, r.dtype) for r in results], pltpu.SemaphoreType.DMA((2, 4))],
        compiler_params=pltpu.CompilerParams(vmem_limit_bytes=62 * 2**20),
    )(*results)


def solution(mesh):
    return jax.shard_map(
        on_device,
        mesh=mesh,
        in_specs=(
            P("ffn", "seq"),
            P("ffn", "seq"),
            P("seq", "ffn"),
            P("seq", "ffn"),
            P("ffn", "seq"),
            P("seq", "ffn"),
            P("seq", "ffn"),
            P("ffn", "seq"),
        ),
        out_specs=(P("ffn", "seq"), P("seq", "ffn"), P("seq", "ffn"), P("ffn", "seq")),
        check_vma=False,
    )
```

```python
import jax
import jax.numpy as jnp
from jax import lax
from jax.experimental import pallas as pl
from jax.experimental.pallas import tpu as pltpu
from jax.sharding import PartitionSpec as P

BF = jnp.bfloat16
F32 = jnp.float32
MESH = pl.DeviceIdType.MESH
RELATIONS = (0, 1, 2, 3)


def partner(i, relation):
    if relation == 0:
        return i
    if relation == 1:
        return lax.rem(5 - i, 4)
    if relation == 2:
        return 3 - i
    return lax.rem(i + 2, 4)


def rows16(y):
    return pl.ds(pl.multiple_of(y * 16, 16), 16)


def matmul(left, right):
    return jnp.dot(left, right, preferred_element_type=F32)


def kernel(
    t_ref, g_ref, wg_ref, wu_ref, wd_ref, mgt_ref, mut_ref, mdt_ref,
    out_ref, gg_ref, gu_ref, gd_ref,
    wg_raw, wu_raw, wd_raw, mg, mu, md, xf, xt, gf, wgu, wd, wdp,
    gu_send, gu_keep, gu_core, gu_zs, gu_zk, gu_r1, gu_z2, gu_r2, gu_own,
    dh_send, dh_keep, dh_core, dh_zs, dh_zk, dh_r1, dh_z2, dh_r2,
    hf, df,
    oa_own, oa_send, oa_recv, ob_own, ob_send, ob_recv,
    a2_own, a2_send, a2_recv, b2_own, b2_send, b2_recv, o3, o3_send, o3_recv,
    send_sem, recv_sem, load_sem,
):
    seq = lax.axis_index("seq")
    ffn = lax.axis_index("ffn")
    zh, core = seq // 2, lax.rem(seq, 2)
    x, zl, y = ffn // 16, lax.rem(ffn // 4, 4), lax.rem(ffn, 4)
    other = 1 - core

    def ffn_peer(rx, rz, ry):
        return (seq, partner(x, rx) * 16 + partner(zl, rz) * 4 + partner(y, ry))

    def zh_peer(relation):
        return (partner(zh, relation) * 2 + core, ffn)

    core_peer = (zh * 2 + other, ffn)

    peers = [ffn_peer(*r) for m in (1, 2, 3) for r in ((m, 0, 0), (0, m, 0), (0, 0, m))]
    peers += [core_peer, zh_peer(1), zh_peer(2)]
    barrier = pltpu.get_barrier_semaphore()
    for peer in peers:
        pl.semaphore_signal(barrier, inc=1, device_id=peer, device_id_type=MESH)

    started = []

    def send(src, dst, peer):
        index = len(started)
        copy = pltpu.make_async_remote_copy(
            src_ref=src, dst_ref=dst, send_sem=send_sem.at[index], recv_sem=recv_sem.at[index],
            device_id=peer, device_id_type=MESH,
        )
        copy.start()
        started.append(copy)
        return copy

    x_own, g_own = xf.at[x, zl, rows16(y)], gf.at[x, zl, rows16(y)]
    loads = [
        pltpu.make_async_copy(src, dst, load_sem.at[i])
        for i, (src, dst) in enumerate((
            (t_ref, x_own), (g_ref, g_own), (mgt_ref, mg), (mut_ref, mu), (mdt_ref, md),
            (wg_ref, wg_raw), (wu_ref, wu_raw), (wd_ref, wd_raw),
        ))
    ]
    for load in loads:
        load.start()
    for load in loads:
        load.wait()

    for b in range(2):
        place = lax.rem(b + core, 2)
        for a in range(4):
            r, c = pl.ds(a * 128, 128), pl.ds(b * 128, 128)
            for t, (raw, mask) in enumerate(((wg_raw, mg), (wu_raw, mu))):
                kept = (raw[r, c].astype(F32) * mask[b, a].astype(F32)).astype(BF)
                wgu[r, pl.ds(pl.multiple_of(place * 256 + t * 128, 128), 128)] = kept
            kept = (wd_raw[c, r].astype(F32) * md[b, a].astype(F32)).astype(BF)
            wd[c, r] = kept
            wdp[pl.ds(pl.multiple_of(place * 128, 128), 128), r] = kept

    pl.semaphore_wait(barrier, len(peers))

    def landed(*copies):
        for copy in copies:
            if not any(copy is old for old in arrived):
                arrived.append(copy)
                copy.wait_recv()

    arrived = []
    x_z = [send(x_own, x_own, ffn_peer(0, r, 0)) for r in (1, 2, 3)]
    g_z = [send(g_own, g_own, ffn_peer(0, r, 0)) for r in (1, 2, 3)]
    x_flow, g_flow = {}, {}
    left, right = pl.ds(0, 256), pl.ds(256, 256)

    def spread(column, rows, flow):
        landed(*column)
        a, b = rows.at[x, :, rows16(y)], rows.at[x, :, rows16(y), right]
        flow[0] = [send(a, a, ffn_peer(0, 0, r)) for r in (1, 2, 3)]
        flow["b"] = [send(b, b, ffn_peer(r, 0, 0)) for r in (1, 2, 3)]

    def complete(rows, flow):
        for j in (1, 2, 3):
            landed(flow["b"][j - 1])
            b = rows.at[partner(x, j), :, rows16(y), right]
            flow[j] = [send(b, b, ffn_peer(0, 0, r)) for r in (1, 2, 3)]
        landed(*flow[0])
        a = rows.at[x, :, :, left]
        for j in (1, 2, 3):
            flow[j].append(send(a, a, ffn_peer(j, 0, 0)))

    gu = dict(send=gu_send, keep=gu_keep, core=gu_core, zs=gu_zs, zk=gu_zk, r1=gu_r1, z2=gu_z2,
              r2=gu_r2, n=2, c1={}, c2={}, c3={})
    dh = dict(send=dh_send, keep=dh_keep, core=dh_core, zs=dh_zs, zk=dh_zk, r1=dh_r1, z2=dh_z2,
              r2=dh_r2, n=1, c1={}, c2={}, c3={})

    def to_core(k, j, both):
        n = k["n"]
        for t in range(n):
            k["send"][j, t] = both[:, 128 * (n + t):128 * (n + t + 1)].reshape(4, 64, 128).astype(BF)
            k["keep"][j, t] = both[:, 128 * t:128 * (t + 1)].reshape(4, 64, 128)
        k["c1"][j] = send(k["send"].at[j], k["core"].at[j], core_peer)

    def to_z1(k, j):
        k["c1"][j].wait_recv()
        k["c2"][j] = []
        for h in (0, 1):
            r = pl.ds(32 * h, 32)
            first, second = (1, 2) if h == 0 else (2, 1)
            for t in range(k["n"]):
                for slot, (keep, relation) in enumerate(
                    ((False, first), (False, 3), (True, 0), (True, second))
                ):
                    b = partner(zh, relation)
                    value = k["keep"][j, t, b, r, :] + k["core"][j, t, b, r, :].astype(F32)
                    if keep:
                        k["zk"][j, h, t, slot - 2] = value
                    else:
                        k["zs"][j, h, t, slot] = value.astype(BF)
            k["c2"][j].append(send(k["zs"].at[j, h], k["r1"].at[j, h], zh_peer(first)))

    def to_z2(k, j):
        k["c3"][j] = []
        for h in (0, 1):
            k["c2"][j][h].wait_recv()
            for t in range(k["n"]):
                k["z2"][j, h, t] = (k["zk"][j, h, t, 1] + k["r1"][j, h, t, 1].astype(F32)).astype(BF)
            k["c3"][j].append(send(k["z2"].at[j, h], k["r2"].at[j, h], zh_peer(2 if h == 0 else 1)))

    def owned(k, j, h, t):
        return (
            k["zk"][j, h, t, 0] + k["r1"][j, h, t, 0].astype(F32) + k["r2"][j, h, t].astype(F32)
        )

    def gather1(full, j):
        mine = full.at[j, core, :, zh]
        return [send(mine, mine, zh_peer(r)) for r in (1, 2)]

    def gather2(full, j, copies):
        result = []
        for h, (relation, onward) in enumerate(((1, 2), (2, 1))):
            copies[h].wait_recv()
            block = full.at[j, core, :, partner(zh, relation), pl.ds(32 * h, 32)]
            result.append(send(block, block, zh_peer(onward)))
        return result

    def gather3(full, j, copies):
        for copy in copies:
            copy.wait_recv()
        return send(full.at[j, core], full.at[j, core], core_peer)

    def gu_compute(j):
        landed(*x_flow[j])
        to_core(gu, j, matmul(xf[partner(x, j)].reshape(256, 512), wgu[...]))

    def transpose_x(j):
        xt[j] = xf[partner(x, j)].reshape(256, 512).T

    h1, h2, h3, d1, d2, d3 = ({} for _ in range(6))

    def gu_final(j):
        for h in (0, 1):
            gu["c3"][j][h].wait_recv()
            gate, up = owned(gu, j, h, 0), owned(gu, j, h, 1)
            sig = 1.0 / (1.0 + jnp.exp(-gate))
            hf[j, core, 0, zh, pl.ds(32 * h, 32), :] = (gate * sig * up).astype(BF)
            gu_own[j, h, 0] = gate
            gu_own[j, h, 1] = up
        h1[j] = gather1(hf, j)

    def dh_compute(j):
        landed(*g_flow[j])
        chunk = gf[partner(x, j)].reshape(256, 512)
        to_core(dh, j, lax.dot_general(
            chunk, wdp[...], (((1,), (1,)), ((), ())), preferred_element_type=F32
        ))

    def dh_final(j):
        for h in (0, 1):
            dh["c3"][j][h].wait_recv()
            d_hidden, gate, up = owned(dh, j, h, 0), gu_own[j, h, 0], gu_own[j, h, 1]
            sig = 1.0 / (1.0 + jnp.exp(-gate))
            d_gate = d_hidden * up * sig * (1.0 + gate * (1.0 - sig))
            d_up = d_hidden * (gate * sig)
            df[j, core, 0, zh, pl.ds(32 * h, 32), :] = d_gate.astype(BF)
            df[j, core, 1, zh, pl.ds(32 * h, 32), :] = d_up.astype(BF)
        d1[j] = gather1(df, j)

    def h_go2(j):
        h2[j] = gather2(hf, j, h1[j])

    def h_go3(j):
        h3[j] = gather3(hf, j, h2[j])

    def d_go2(j):
        d2[j] = gather2(df, j, d1[j])

    def d_go3(j):
        d3[j] = gather3(df, j, d2[j])

    oa, ob = {}, {}
    h_done, d_done = [], []
    h_done, d_done = [], []

    def h_final(j):
        h3[j].wait_recv()
        hidden = jnp.concatenate(
            [hf[j, 0, 0].reshape(256, 128), hf[j, 1, 0].reshape(256, 128)], axis=1
        )
        part = matmul(hidden, wd[...])
        a, b = part[:, :256].reshape(4, 64, 256), part[:, 256:].reshape(4, 64, 256)
        if j == 0:
            oa_own[...] = a
        else:
            oa_send[j - 1] = a.astype(BF)
            oa[j] = send(oa_send.at[j - 1], oa_recv.at[j - 1], ffn_peer(j, 0, 0))
        ob_send[j] = b.astype(BF)
        ob[j] = [
            send(ob_send.at[j, :, rows16(partner(y, r))], ob_recv.at[j, r - 1], ffn_peer(0, 0, r))
            for r in (1, 2, 3)
        ]
        chunk = gf[partner(x, j)].reshape(256, 512)
        term = lax.dot_general(hidden, chunk, (((0,), (0,)), ((), ())), preferred_element_type=F32)
        if h_done:
            term += gd_ref[...]
        h_done.append(j)
        if len(h_done) < 4:
            gd_ref[...] = term
            return
        for a in range(2):
            for b in range(4):
                r, c = slice(a * 128, a * 128 + 128), slice(b * 128, b * 128 + 128)
                gd_ref[r, c] = term[r, c] * md[a, b].astype(F32)

    a2, b2, z3 = {}, {}, {}

    def out_second():
        for j in (1, 2, 3):
            oa[j].wait_recv()
        total = oa_own[...]
        for j in range(3):
            total += oa_recv[j].astype(F32)
        oa_own[...] = total
        a2_send[...] = total.astype(BF)
        for r in (1, 2, 3):
            a2[r] = send(a2_send.at[:, rows16(partner(y, r))], a2_recv.at[r - 1], ffn_peer(0, 0, r))
        for j in range(4):
            for copy in ob[j]:
                copy.wait_recv()
            total = ob_send[j, :, rows16(y), :].astype(F32)
            for r in range(3):
                total += ob_recv[j, r].astype(F32)
            if j == 0:
                b2_own[...] = total
            else:
                b2_send[j - 1] = total.astype(BF)
                b2[j] = send(b2_send.at[j - 1], b2_recv.at[j - 1], ffn_peer(j, 0, 0))

    def out_third():
        for r in (1, 2, 3):
            a2[r].wait_recv()
            b2[r].wait_recv()
        left, right = oa_own[:, rows16(y), :], b2_own[...]
        for r in range(3):
            left += a2_recv[r].astype(F32)
            right += b2_recv[r].astype(F32)
        o3[:, :, :256] = left
        o3[:, :, 256:] = right
        o3_send[...] = o3[...].astype(BF)
        for r in (1, 2, 3):
            z3[r] = send(o3_send.at[partner(zl, r)], o3_recv.at[r - 1], ffn_peer(0, r, 0))

    def out_final():
        total = o3[zl]
        for r in (1, 2, 3):
            z3[r].wait_recv()
            total += o3_recv[r - 1].astype(F32)
        out_ref[...] = total.astype(BF)

    def d_final(j):
        d3[j].wait_recv()
        for t, (ref, mask) in enumerate(((gg_ref, mg), (gu_ref, mu))):
            grad = jnp.concatenate(
                [df[j, 0, t].reshape(256, 128), df[j, 1, t].reshape(256, 128)], axis=1
            )
            term = matmul(xt[j], grad)
            if d_done:
                term += ref[...]
            if len(d_done) < 3:
                ref[...] = term
                continue
            for a in range(4):
                for b in range(2):
                    r, c = slice(a * 128, a * 128 + 128), slice(b * 128, b * 128 + 128)
                    ref[r, c] = term[r, c] * mask[b, a].astype(F32)
        d_done.append(j)
        d_done.append(j)

    spread(x_z, xf, x_flow)
    complete(xf, x_flow)
    gu_compute(0)
    to_z1(gu, 0)
    gu_compute(1)
    gu_compute(2)
    gu_compute(3)
    spread(g_z, gf, g_flow)
    to_z1(gu, 1)
    to_z1(gu, 2)
    to_z1(gu, 3)
    complete(gf, g_flow)
    to_z2(gu, 0)
    transpose_x(0)
    transpose_x(1)
    to_z2(gu, 1)
    transpose_x(2)
    transpose_x(3)
    to_z2(gu, 2)
    dh_compute(0)
    dh_compute(1)
    dh_compute(2)
    dh_compute(3)
    to_z2(gu, 3)
    to_z1(dh, 0)
    to_z1(dh, 1)
    to_z1(dh, 2)
    to_z1(dh, 3)
    gu_final(0)
    gu_final(1)
    gu_final(2)
    gu_final(3)
    to_z2(dh, 0)
    to_z2(dh, 1)
    to_z2(dh, 2)
    to_z2(dh, 3)
    h_go2(0)
    h_go2(1)
    h_go2(2)
    h_go2(3)
    dh_final(0)
    dh_final(1)
    dh_final(2)
    dh_final(3)
    h_go3(0)
    h_go3(1)
    h_go3(2)
    h_final(0)
    h_go3(3)
    h_final(1)
    h_final(2)
    h_final(3)
    d_go2(0)
    d_go2(1)
    out_second()
    d_go2(2)
    d_go2(3)
    out_third()
    d_go3(0)
    d_go3(1)
    d_final(0)
    d_go3(2)
    d_final(1)
    d_go3(3)
    out_final()
    d_final(2)
    d_final(3)
    for copy in started:
        copy.wait_send()


def hand_over(*refs):
    source, result, held, sem = refs[:4], refs[4:8], refs[8:12], refs[12]
    loads = [pltpu.make_async_copy(source[i], held[i], sem.at[0, i]) for i in range(4)]
    stores = [pltpu.make_async_copy(held[i], result[i], sem.at[1, i]) for i in range(4)]
    for load in loads:
        load.start()
    for load, store in zip(loads, stores):
        load.wait()
        store.start()
    for store in stores:
        store.wait()


def reduce_scratch(n):
    return [
        pltpu.VMEM((4, n, 4, 64, 128), BF),
        pltpu.VMEM((4, n, 4, 64, 128), F32),
        pltpu.VMEM((4, n, 4, 64, 128), BF),
        pltpu.VMEM((4, 2, n, 2, 32, 128), BF),
        pltpu.VMEM((4, 2, n, 2, 32, 128), F32),
        pltpu.VMEM((4, 2, n, 2, 32, 128), BF),
        pltpu.VMEM((4, 2, n, 32, 128), BF),
        pltpu.VMEM((4, 2, n, 32, 128), BF),
    ]


COPIES = 160


def on_device(teacher_rows, grad_out, w_gate, w_up, w_down, mask_gate, mask_up, mask_down):
    args = (teacher_rows, grad_out, w_gate, w_up, w_down, mask_gate.T, mask_up.T, mask_down)
    vmem = pl.BlockSpec(memory_space=pltpu.VMEM)
    hbm = pl.BlockSpec(memory_space=pltpu.HBM)
    results = pl.pallas_call(
        kernel,
        out_shape=(
            jax.ShapeDtypeStruct((16, 512), BF),
            jax.ShapeDtypeStruct((512, 256), F32),
            jax.ShapeDtypeStruct((512, 256), F32),
            jax.ShapeDtypeStruct((256, 512), F32),
        ),
        in_specs=[hbm] * 8,
        out_specs=(vmem,) * 4,
        scratch_shapes=[
            pltpu.VMEM((512, 256), BF),
            pltpu.VMEM((512, 256), BF),
            pltpu.VMEM((256, 512), BF),
            *[pltpu.SMEM((2, 4), jnp.int32)] * 3,
            pltpu.VMEM((4, 4, 64, 512), BF),
            pltpu.VMEM((4, 512, 256), BF),
            pltpu.VMEM((4, 4, 64, 512), BF),
            pltpu.VMEM((512, 512), BF),
            pltpu.VMEM((256, 512), BF),
            pltpu.VMEM((256, 512), BF),
            *reduce_scratch(2),
            pltpu.VMEM((4, 2, 2, 32, 128), F32),
            *reduce_scratch(1),
            pltpu.VMEM((4, 2, 1, 4, 64, 128), BF),
            pltpu.VMEM((4, 2, 2, 4, 64, 128), BF),
            pltpu.VMEM((4, 64, 256), F32),
            pltpu.VMEM((3, 4, 64, 256), BF),
            pltpu.VMEM((3, 4, 64, 256), BF),
            pltpu.VMEM((4, 16, 256), F32),
            pltpu.VMEM((4, 4, 64, 256), BF),
            pltpu.VMEM((4, 3, 4, 16, 256), BF),
            pltpu.VMEM((4, 16, 256), F32),
            pltpu.VMEM((4, 64, 256), BF),
            pltpu.VMEM((3, 4, 16, 256), BF),
            pltpu.VMEM((4, 16, 256), F32),
            pltpu.VMEM((3, 4, 16, 256), BF),
            pltpu.VMEM((3, 4, 16, 256), BF),
            pltpu.VMEM((4, 16, 512), F32),
            pltpu.VMEM((4, 16, 512), BF),
            pltpu.VMEM((3, 16, 512), BF),
            pltpu.SemaphoreType.DMA((COPIES,)),
            pltpu.SemaphoreType.DMA((COPIES,)),
            pltpu.SemaphoreType.DMA((8,)),
        ],
        compiler_params=pltpu.CompilerParams(
            collective_id=0, has_side_effects=True, vmem_limit_bytes=62 * 2**20
        ),
        cost_estimate=pl.CostEstimate(flops=1_700_000_000, bytes_accessed=2_500_000, transcendentals=100_000),
    )(*args)
    return pl.pallas_call(
        hand_over,
        out_shape=tuple(jax.ShapeDtypeStruct(r.shape, r.dtype) for r in results),
        in_specs=[hbm] * 4,
        out_specs=(hbm,) * 4,
        scratch_shapes=[*[pltpu.VMEM(r.shape, r.dtype) for r in results], pltpu.SemaphoreType.DMA((2, 4))],
        compiler_params=pltpu.CompilerParams(vmem_limit_bytes=62 * 2**20),
    )(*results)


def solution(mesh):
    return jax.shard_map(
        on_device,
        mesh=mesh,
        in_specs=(
            P("ffn", "seq"),
            P("ffn", "seq"),
            P("seq", "ffn"),
            P("seq", "ffn"),
            P("ffn", "seq"),
            P("seq", "ffn"),
            P("seq", "ffn"),
            P("ffn", "seq"),
        ),
        out_specs=(P("ffn", "seq"), P("seq", "ffn"), P("seq", "ffn"), P("ffn", "seq")),
        check_vma=False,
    )
```

```python
import jax
import jax.numpy as jnp
from jax import lax
from jax.experimental import pallas as pl
from jax.experimental.pallas import tpu as pltpu
from jax.sharding import PartitionSpec as P

BF = jnp.bfloat16
F32 = jnp.float32
MESH = pl.DeviceIdType.MESH
RELATIONS = (0, 1, 2, 3)


def partner(i, relation):
    if relation == 0:
        return i
    if relation == 1:
        return lax.rem(5 - i, 4)
    if relation == 2:
        return 3 - i
    return lax.rem(i + 2, 4)


def rows16(y):
    return pl.ds(pl.multiple_of(y * 16, 16), 16)


def matmul(left, right):
    return jnp.dot(left, right, preferred_element_type=F32)


def kernel(
    t_ref, g_ref, wg_ref, wu_ref, wd_ref, mgt_ref, mut_ref, mdt_ref,
    out_ref, gg_ref, gu_ref, gd_ref,
    wg_raw, wu_raw, wd_raw, mg, mu, md, xf, xt, gf, wgu, wd, wdp,
    gu_send, gu_keep, gu_core, gu_zs, gu_zk, gu_r1, gu_z2, gu_r2, gu_own,
    dh_send, dh_keep, dh_core, dh_zs, dh_zk, dh_r1, dh_z2, dh_r2,
    hf, df,
    oa_own, oa_send, oa_recv, ob_own, ob_send, ob_recv,
    a2_own, a2_send, a2_recv, b2_own, b2_send, b2_recv, o3, o3_send, o3_recv,
    send_sem, recv_sem, load_sem,
):
    seq = lax.axis_index("seq")
    ffn = lax.axis_index("ffn")
    zh, core = seq // 2, lax.rem(seq, 2)
    x, zl, y = ffn // 16, lax.rem(ffn // 4, 4), lax.rem(ffn, 4)
    other = 1 - core

    def ffn_peer(rx, rz, ry):
        return (seq, partner(x, rx) * 16 + partner(zl, rz) * 4 + partner(y, ry))

    def zh_peer(relation):
        return (partner(zh, relation) * 2 + core, ffn)

    core_peer = (zh * 2 + other, ffn)

    peers = [ffn_peer(*r) for m in (1, 2, 3) for r in ((m, 0, 0), (0, m, 0), (0, 0, m))]
    peers += [core_peer, zh_peer(1), zh_peer(2)]
    barrier = pltpu.get_barrier_semaphore()
    for peer in peers:
        pl.semaphore_signal(barrier, inc=1, device_id=peer, device_id_type=MESH)

    started = []

    def send(src, dst, peer):
        index = len(started)
        copy = pltpu.make_async_remote_copy(
            src_ref=src, dst_ref=dst, send_sem=send_sem.at[index], recv_sem=recv_sem.at[index],
            device_id=peer, device_id_type=MESH,
        )
        copy.start()
        started.append(copy)
        return copy

    x_own, g_own = xf.at[x, zl, rows16(y)], gf.at[x, zl, rows16(y)]
    loads = [
        pltpu.make_async_copy(src, dst, load_sem.at[i])
        for i, (src, dst) in enumerate((
            (t_ref, x_own), (g_ref, g_own), (mgt_ref, mg), (mut_ref, mu), (mdt_ref, md),
            (wg_ref, wg_raw), (wu_ref, wu_raw), (wd_ref, wd_raw),
        ))
    ]
    for load in loads:
        load.start()
    for load in loads[:2]:
        load.wait()

    pl.semaphore_wait(barrier, len(peers))

    def landed(*copies):
        for copy in copies:
            if not any(copy is old for old in arrived):
                arrived.append(copy)
                copy.wait_recv()

    arrived = []
    x_z = [send(x_own, x_own, ffn_peer(0, r, 0)) for r in (1, 2, 3)]
    g_z = [send(g_own, g_own, ffn_peer(0, r, 0)) for r in (1, 2, 3)]

    for load in loads[2:]:
        load.wait()

    for b in range(2):
        place = lax.rem(b + core, 2)
        for a in range(4):
            r, c = pl.ds(a * 128, 128), pl.ds(b * 128, 128)
            for t, (raw, mask) in enumerate(((wg_raw, mg), (wu_raw, mu))):
                kept = (raw[r, c].astype(F32) * mask[b, a].astype(F32)).astype(BF)
                wgu[r, pl.ds(pl.multiple_of(place * 256 + t * 128, 128), 128)] = kept
            kept = (wd_raw[c, r].astype(F32) * md[b, a].astype(F32)).astype(BF)
            wd[c, r] = kept
            wdp[pl.ds(pl.multiple_of(place * 128, 128), 128), r] = kept

    x_flow, g_flow = {}, {}
    left, right = pl.ds(0, 256), pl.ds(256, 256)

    def spread(column, rows, flow):
        landed(*column)
        a, b = rows.at[x, :, rows16(y)], rows.at[x, :, rows16(y), right]
        flow[0] = [send(a, a, ffn_peer(0, 0, r)) for r in (1, 2, 3)]
        flow["b"] = [send(b, b, ffn_peer(r, 0, 0)) for r in (1, 2, 3)]

    def complete(rows, flow, chunks):
        for j in chunks:
            landed(flow["b"][j - 1])
            b = rows.at[partner(x, j), :, rows16(y), right]
            flow[j] = [send(b, b, ffn_peer(0, 0, r)) for r in (1, 2, 3)]
        landed(*flow[0])
        a = rows.at[x, :, :, left]
        for j in chunks:
            flow[j].append(send(a, a, ffn_peer(j, 0, 0)))

    gu = dict(send=gu_send, keep=gu_keep, core=gu_core, zs=gu_zs, zk=gu_zk, r1=gu_r1, z2=gu_z2,
              r2=gu_r2, n=2, c1={}, c2={}, c3={})
    dh = dict(send=dh_send, keep=dh_keep, core=dh_core, zs=dh_zs, zk=dh_zk, r1=dh_r1, z2=dh_z2,
              r2=dh_r2, n=1, c1={}, c2={}, c3={})

    def to_core(k, j, both):
        n = k["n"]
        for t in range(n):
            k["send"][j, t] = both[:, 128 * (n + t):128 * (n + t + 1)].reshape(4, 64, 128).astype(BF)
            k["keep"][j, t] = both[:, 128 * t:128 * (t + 1)].reshape(4, 64, 128)
        k["c1"][j] = send(k["send"].at[j], k["core"].at[j], core_peer)

    def to_z1(k, j):
        k["c1"][j].wait_recv()
        k["c2"][j] = []
        for h in (0, 1):
            r = pl.ds(32 * h, 32)
            first, second = (1, 2) if h == 0 else (2, 1)
            for t in range(k["n"]):
                for slot, (keep, relation) in enumerate(
                    ((False, first), (False, 3), (True, 0), (True, second))
                ):
                    b = partner(zh, relation)
                    value = k["keep"][j, t, b, r, :] + k["core"][j, t, b, r, :].astype(F32)
                    if keep:
                        k["zk"][j, h, t, slot - 2] = value
                    else:
                        k["zs"][j, h, t, slot] = value.astype(BF)
            k["c2"][j].append(send(k["zs"].at[j, h], k["r1"].at[j, h], zh_peer(first)))

    def to_z2(k, j):
        k["c3"][j] = []
        for h in (0, 1):
            k["c2"][j][h].wait_recv()
            for t in range(k["n"]):
                k["z2"][j, h, t] = (k["zk"][j, h, t, 1] + k["r1"][j, h, t, 1].astype(F32)).astype(BF)
            k["c3"][j].append(send(k["z2"].at[j, h], k["r2"].at[j, h], zh_peer(2 if h == 0 else 1)))

    def owned(k, j, h, t):
        return (
            k["zk"][j, h, t, 0] + k["r1"][j, h, t, 0].astype(F32) + k["r2"][j, h, t].astype(F32)
        )

    def gather1(full, j):
        mine = full.at[j, core, :, zh]
        return [send(mine, mine, zh_peer(r)) for r in (1, 2)]

    def gather2(full, j, copies):
        result = []
        for h, (relation, onward) in enumerate(((1, 2), (2, 1))):
            copies[h].wait_recv()
            block = full.at[j, core, :, partner(zh, relation), pl.ds(32 * h, 32)]
            result.append(send(block, block, zh_peer(onward)))
        return result

    def gather3(full, j, copies):
        for copy in copies:
            copy.wait_recv()
        return send(full.at[j, core], full.at[j, core], core_peer)

    def gu_compute(j):
        landed(*x_flow[j])
        to_core(gu, j, matmul(xf[partner(x, j)].reshape(256, 512), wgu[...]))

    def transpose_x(j):
        xt[j] = xf[partner(x, j)].reshape(256, 512).T

    h1, h2, h3, d1, d2, d3 = ({} for _ in range(6))

    def gu_final(j):
        for h in (0, 1):
            gu["c3"][j][h].wait_recv()
            gate, up = owned(gu, j, h, 0), owned(gu, j, h, 1)
            sig = 1.0 / (1.0 + jnp.exp(-gate))
            hf[j, core, 0, zh, pl.ds(32 * h, 32), :] = (gate * sig * up).astype(BF)
            gu_own[j, h, 0] = gate
            gu_own[j, h, 1] = up
        h1[j] = gather1(hf, j)

    def dh_compute(j):
        landed(*g_flow[j])
        chunk = gf[partner(x, j)].reshape(256, 512)
        to_core(dh, j, lax.dot_general(
            chunk, wdp[...], (((1,), (1,)), ((), ())), preferred_element_type=F32
        ))

    def dh_final(j):
        for h in (0, 1):
            dh["c3"][j][h].wait_recv()
            d_hidden, gate, up = owned(dh, j, h, 0), gu_own[j, h, 0], gu_own[j, h, 1]
            sig = 1.0 / (1.0 + jnp.exp(-gate))
            d_gate = d_hidden * up * sig * (1.0 + gate * (1.0 - sig))
            d_up = d_hidden * (gate * sig)
            df[j, core, 0, zh, pl.ds(32 * h, 32), :] = d_gate.astype(BF)
            df[j, core, 1, zh, pl.ds(32 * h, 32), :] = d_up.astype(BF)
        d1[j] = gather1(df, j)

    def h_go2(j):
        h2[j] = gather2(hf, j, h1[j])

    def h_go3(j):
        h3[j] = gather3(hf, j, h2[j])

    def d_go2(j):
        d2[j] = gather2(df, j, d1[j])

    def d_go3(j):
        d3[j] = gather3(df, j, d2[j])

    oa, ob = {}, {}
    h_done, d_done = [], []
    h_done, d_done = [], []

    def h_final(j):
        h3[j].wait_recv()
        hidden = jnp.concatenate(
            [hf[j, 0, 0].reshape(256, 128), hf[j, 1, 0].reshape(256, 128)], axis=1
        )
        part = matmul(hidden, wd[...])
        a, b = part[:, :256].reshape(4, 64, 256), part[:, 256:].reshape(4, 64, 256)
        if j == 0:
            oa_own[...] = a
        else:
            oa_send[j - 1] = a.astype(BF)
            oa[j] = send(oa_send.at[j - 1], oa_recv.at[j - 1], ffn_peer(j, 0, 0))
        ob_send[j] = b.astype(BF)
        ob[j] = [
            send(ob_send.at[j, :, rows16(partner(y, r))], ob_recv.at[j, r - 1], ffn_peer(0, 0, r))
            for r in (1, 2, 3)
        ]
        chunk = gf[partner(x, j)].reshape(256, 512)
        term = lax.dot_general(hidden, chunk, (((0,), (0,)), ((), ())), preferred_element_type=F32)
        if h_done:
            term += gd_ref[...]
        h_done.append(j)
        if len(h_done) < 4:
            gd_ref[...] = term
            return
        for a in range(2):
            for b in range(4):
                r, c = slice(a * 128, a * 128 + 128), slice(b * 128, b * 128 + 128)
                gd_ref[r, c] = term[r, c] * md[a, b].astype(F32)

    a2, b2, z3 = {}, {}, {}

    def out_second():
        for j in (1, 2, 3):
            oa[j].wait_recv()
        total = oa_own[...]
        for j in range(3):
            total += oa_recv[j].astype(F32)
        oa_own[...] = total
        a2_send[...] = total.astype(BF)
        for r in (1, 2, 3):
            a2[r] = send(a2_send.at[:, rows16(partner(y, r))], a2_recv.at[r - 1], ffn_peer(0, 0, r))
        for j in range(4):
            for copy in ob[j]:
                copy.wait_recv()
            total = ob_send[j, :, rows16(y), :].astype(F32)
            for r in range(3):
                total += ob_recv[j, r].astype(F32)
            if j == 0:
                b2_own[...] = total
            else:
                b2_send[j - 1] = total.astype(BF)
                b2[j] = send(b2_send.at[j - 1], b2_recv.at[j - 1], ffn_peer(j, 0, 0))

    def out_third():
        for r in (1, 2, 3):
            a2[r].wait_recv()
            b2[r].wait_recv()
        left, right = oa_own[:, rows16(y), :], b2_own[...]
        for r in range(3):
            left += a2_recv[r].astype(F32)
            right += b2_recv[r].astype(F32)
        o3[:, :, :256] = left
        o3[:, :, 256:] = right
        o3_send[...] = o3[...].astype(BF)
        for r in (1, 2, 3):
            z3[r] = send(o3_send.at[partner(zl, r)], o3_recv.at[r - 1], ffn_peer(0, r, 0))

    def out_final():
        total = o3[zl]
        for r in (1, 2, 3):
            z3[r].wait_recv()
            total += o3_recv[r - 1].astype(F32)
        out_ref[...] = total.astype(BF)

    def d_final(j):
        d3[j].wait_recv()
        for t, (ref, mask) in enumerate(((gg_ref, mg), (gu_ref, mu))):
            grad = jnp.concatenate(
                [df[j, 0, t].reshape(256, 128), df[j, 1, t].reshape(256, 128)], axis=1
            )
            term = matmul(xt[j], grad)
            if d_done:
                term += ref[...]
            if len(d_done) < 3:
                ref[...] = term
                continue
            for a in range(4):
                for b in range(2):
                    r, c = slice(a * 128, a * 128 + 128), slice(b * 128, b * 128 + 128)
                    ref[r, c] = term[r, c] * mask[b, a].astype(F32)
        d_done.append(j)
        d_done.append(j)

    spread(x_z, xf, x_flow)
    complete(xf, x_flow, (1, 2))
    gu_compute(0)
    to_z1(gu, 0)
    gu_compute(1)
    complete(xf, x_flow, (3,))
    gu_compute(2)
    to_z1(gu, 1)
    to_z1(gu, 2)
    gu_compute(3)
    spread(g_z, gf, g_flow)
    to_z1(gu, 3)
    complete(gf, g_flow, (1, 2, 3))
    to_z2(gu, 0)
    transpose_x(0)
    transpose_x(1)
    to_z2(gu, 1)
    transpose_x(2)
    transpose_x(3)
    to_z2(gu, 2)
    dh_compute(0)
    dh_compute(1)
    dh_compute(2)
    dh_compute(3)
    to_z2(gu, 3)
    to_z1(dh, 0)
    to_z1(dh, 1)
    to_z1(dh, 2)
    to_z1(dh, 3)
    gu_final(0)
    gu_final(1)
    gu_final(2)
    gu_final(3)
    to_z2(dh, 0)
    to_z2(dh, 1)
    to_z2(dh, 2)
    to_z2(dh, 3)
    h_go2(0)
    h_go2(1)
    h_go2(2)
    h_go2(3)
    dh_final(0)
    dh_final(1)
    dh_final(2)
    dh_final(3)
    h_go3(0)
    h_go3(1)
    h_go3(2)
    h_final(0)
    h_go3(3)
    h_final(1)
    h_final(2)
    h_final(3)
    d_go2(0)
    d_go2(1)
    out_second()
    d_go2(2)
    d_go2(3)
    out_third()
    d_go3(0)
    d_go3(1)
    d_final(0)
    d_go3(2)
    d_final(1)
    d_go3(3)
    out_final()
    d_final(2)
    d_final(3)
    for copy in started:
        copy.wait_send()


def hand_over(*refs):
    source, result, held, sem = refs[:4], refs[4:8], refs[8:12], refs[12]
    loads = [pltpu.make_async_copy(source[i], held[i], sem.at[0, i]) for i in range(4)]
    stores = [pltpu.make_async_copy(held[i], result[i], sem.at[1, i]) for i in range(4)]
    for load in loads:
        load.start()
    for load, store in zip(loads, stores):
        load.wait()
        store.start()
    for store in stores:
        store.wait()


def reduce_scratch(n):
    return [
        pltpu.VMEM((4, n, 4, 64, 128), BF),
        pltpu.VMEM((4, n, 4, 64, 128), F32),
        pltpu.VMEM((4, n, 4, 64, 128), BF),
        pltpu.VMEM((4, 2, n, 2, 32, 128), BF),
        pltpu.VMEM((4, 2, n, 2, 32, 128), F32),
        pltpu.VMEM((4, 2, n, 2, 32, 128), BF),
        pltpu.VMEM((4, 2, n, 32, 128), BF),
        pltpu.VMEM((4, 2, n, 32, 128), BF),
    ]


COPIES = 160


def on_device(teacher_rows, grad_out, w_gate, w_up, w_down, mask_gate, mask_up, mask_down):
    args = (teacher_rows, grad_out, w_gate, w_up, w_down, mask_gate.T, mask_up.T, mask_down)
    vmem = pl.BlockSpec(memory_space=pltpu.VMEM)
    hbm = pl.BlockSpec(memory_space=pltpu.HBM)
    results = pl.pallas_call(
        kernel,
        out_shape=(
            jax.ShapeDtypeStruct((16, 512), BF),
            jax.ShapeDtypeStruct((512, 256), F32),
            jax.ShapeDtypeStruct((512, 256), F32),
            jax.ShapeDtypeStruct((256, 512), F32),
        ),
        in_specs=[hbm] * 8,
        out_specs=(vmem,) * 4,
        scratch_shapes=[
            pltpu.VMEM((512, 256), BF),
            pltpu.VMEM((512, 256), BF),
            pltpu.VMEM((256, 512), BF),
            *[pltpu.SMEM((2, 4), jnp.int32)] * 3,
            pltpu.VMEM((4, 4, 64, 512), BF),
            pltpu.VMEM((4, 512, 256), BF),
            pltpu.VMEM((4, 4, 64, 512), BF),
            pltpu.VMEM((512, 512), BF),
            pltpu.VMEM((256, 512), BF),
            pltpu.VMEM((256, 512), BF),
            *reduce_scratch(2),
            pltpu.VMEM((4, 2, 2, 32, 128), F32),
            *reduce_scratch(1),
            pltpu.VMEM((4, 2, 1, 4, 64, 128), BF),
            pltpu.VMEM((4, 2, 2, 4, 64, 128), BF),
            pltpu.VMEM((4, 64, 256), F32),
            pltpu.VMEM((3, 4, 64, 256), BF),
            pltpu.VMEM((3, 4, 64, 256), BF),
            pltpu.VMEM((4, 16, 256), F32),
            pltpu.VMEM((4, 4, 64, 256), BF),
            pltpu.VMEM((4, 3, 4, 16, 256), BF),
            pltpu.VMEM((4, 16, 256), F32),
            pltpu.VMEM((4, 64, 256), BF),
            pltpu.VMEM((3, 4, 16, 256), BF),
            pltpu.VMEM((4, 16, 256), F32),
            pltpu.VMEM((3, 4, 16, 256), BF),
            pltpu.VMEM((3, 4, 16, 256), BF),
            pltpu.VMEM((4, 16, 512), F32),
            pltpu.VMEM((4, 16, 512), BF),
            pltpu.VMEM((3, 16, 512), BF),
            pltpu.SemaphoreType.DMA((COPIES,)),
            pltpu.SemaphoreType.DMA((COPIES,)),
            pltpu.SemaphoreType.DMA((8,)),
        ],
        compiler_params=pltpu.CompilerParams(
            collective_id=0, has_side_effects=True, vmem_limit_bytes=62 * 2**20
        ),
        cost_estimate=pl.CostEstimate(flops=1_700_000_000, bytes_accessed=2_500_000, transcendentals=100_000),
    )(*args)
    return pl.pallas_call(
        hand_over,
        out_shape=tuple(jax.ShapeDtypeStruct(r.shape, r.dtype) for r in results),
        in_specs=[hbm] * 4,
        out_specs=(hbm,) * 4,
        scratch_shapes=[*[pltpu.VMEM(r.shape, r.dtype) for r in results], pltpu.SemaphoreType.DMA((2, 4))],
        compiler_params=pltpu.CompilerParams(vmem_limit_bytes=62 * 2**20),
    )(*results)


def solution(mesh):
    return jax.shard_map(
        on_device,
        mesh=mesh,
        in_specs=(
            P("ffn", "seq"),
            P("ffn", "seq"),
            P("seq", "ffn"),
            P("seq", "ffn"),
            P("ffn", "seq"),
            P("seq", "ffn"),
            P("seq", "ffn"),
            P("ffn", "seq"),
        ),
        out_specs=(P("ffn", "seq"), P("seq", "ffn"), P("seq", "ffn"), P("ffn", "seq")),
        check_vma=False,
    )
```
